512 devices in a mesh: ka: 8 (over z_lo, core), pair: 64 (over y, z_hi, x).
Axes of the slice: x: 4, y: 8, z: 8 (z_hi: 2, z_lo: 4; z = z_hi * 4 + z_lo), core: 2. Of those that a mesh axis runs over, the one named last changes fastest.
Arguments:
- cond_orbitals: bfloat16 [8, 2048, 8192], P('ka', 'pair'), may hold values from -6 to 6
- cond_energy: float32 [8, 8192], P('ka', 'pair'), may hold values from 0.5 to 8
- val_orbitals: bfloat16 [512, 2048], P(('ka', 'pair')), may hold values from -6 to 6
- val_energy: bfloat16 [512], P(('ka', 'pair')), may hold values from -8 to -0.5
- val_slots: int32 [8, 64, 16], P('ka', 'pair'), may hold values from 0 to 511
- owner_count: int32 [8, 64], P('ka', 'pair'), may hold values from 1 to 16, as said below
Outputs:
- response: float32 [8, 2048, 512], P('ka', 'pair')
The draws below stay inside these ranges and needn't reach their ends.
Inputs may be any that keep to these rules, and one draw needn't show every extreme that they name: `owner_count`: in every lane some owner has exactly 16 live slots.
All inputs are finite; a program needn't handle non-finite values.
Results may differ from the reference program's by a relative error of at most 0.0047.
The reference program's roundings to bfloat16 on the way count: a program that leaves them out, or rounds other values in their place, can miss the bound.
Values may be sent and summed in bfloat16 or wider, within the bound.
No kernel may reach another device: no remote copies, remote signals or barrier semaphores. Data moves between devices by JAX's collectives and lax.ppermute only.
A program may use at most 64 MiB of HBM per device.

```python
import jax
import jax.numpy as jnp
from jax import lax

BC = 128
GA = 16
GB = 128
WIN = 512
SLOTS = 16
GRID = 2048
NC = 8192
NVAL = 512
LANES = 8
N_PAIR = 64


def draw_owner_count(key, part):
    first, second = jax.random.split(key)
    counts = jax.random.randint(first, (LANES, N_PAIR), 1, SLOTS + 1)
    where_full = jax.random.randint(second, (LANES, 1), 0, N_PAIR)
    owners = jnp.arange(N_PAIR, dtype=jnp.int32)[None, :]
    return jnp.where(owners == where_full, SLOTS, counts).astype(jnp.int32)


def touch_ends(array, key, least, largest):
    dims = array.shape
    index_at = [jax.random.randint(jax.random.fold_in(key, axis), (), 0, dims[axis]) for axis in range(len(dims))]
    array = array.at[tuple(index_at)].set(least)
    longest = dims.index(max(dims))
    index_at[longest] = (index_at[longest] + 1) % dims[longest]
    return array.at[tuple(index_at)].set(largest)


def block_scale(key, extent, pieces, smallest, largest):
    level = 1.0
    for position, parts in pieces:
        steps = jax.random.uniform(jax.random.fold_in(jax.random.fold_in(key, 6), position), (parts,), jnp.float32, smallest / len(pieces), largest / len(pieces))
        level = level * jnp.repeat(jnp.exp(steps), extent[position] // parts).reshape((-1,) + (1,) * (len(extent) - 1 - position))
    return level


def normal_values(rng, dims, scale, most, cuts=(), kind=jnp.bfloat16):
    values = jax.random.normal(rng, dims, jnp.float32) * scale
    if len(cuts) > 0:
        values = block_scale(rng, dims, cuts, -0.22, 0.18) * values
    return jnp.clip(values, min=-most, max=most).astype(kind)


def setup_inputs(seed: int = 0) -> dict:
    seeds = jax.random.split(jax.random.key(seed), 7)
    return {
        "cond_orbitals": normal_values(seeds[0], (LANES, GRID, NC), 1.0, 6.0, ((0, 8), (1, 64))),
        "cond_energy": jnp.clip(0.5 + 7.5 * jax.random.uniform(seeds[1], (LANES, NC), jnp.float32) ** block_scale(seeds[1], (LANES, NC), ((0, 8), (1, 64)), -0.2, 0.2), 0.5, 8.0),
        "val_orbitals": normal_values(seeds[2], (NVAL, GRID), 1.0, 6.0, ((0, 512),)),
        "val_energy": jnp.clip(-8.0 + 7.5 * jax.random.uniform(seeds[3], (NVAL,), jnp.float32) ** block_scale(seeds[3], (NVAL,), ((0, 512),), -0.2, 0.2), -8.0, -0.5).astype(jnp.bfloat16),
        "val_slots": touch_ends(jax.random.randint(seeds[4], (LANES, N_PAIR, SLOTS), 0, NVAL), jax.random.fold_in(seeds[4], 1), 0, NVAL - 1).astype(jnp.int32),
        "owner_count": draw_owner_count(jax.random.fold_in(seeds[6], 71), 0),
    }


def cosine_table(length):
    freq = lax.iota(jnp.float32, length)[:, None]
    point = lax.iota(jnp.float32, length)[None, :]
    factor = jnp.where(freq == 0, jnp.sqrt(1.0 / length), jnp.sqrt(2.0 / length))
    return (factor * jnp.cos(jnp.pi * (point + 0.5) * freq / length)).astype(jnp.bfloat16)

def owner_terms(picked, e_pick, live, cond_block, e_cond, table_a, table_b):
    slots = picked.shape[0]
    pair_real = (picked[:, None, :].astype(jnp.float32) * cond_block[None].astype(jnp.float32)).astype(jnp.bfloat16)
    count = slots * cond_block.shape[0]
    rows = pair_real.reshape(count * GA, GB)
    first = jnp.dot(rows, table_b.T, preferred_element_type=jnp.float32).astype(jnp.bfloat16)
    first = first.reshape(count, GA, GB)
    moved = jnp.einsum('ja,pak->pjk', table_a.astype(jnp.float32), first.astype(jnp.float32))
    moved = moved.astype(jnp.bfloat16).reshape(count, GA * GB)
    weight = live[:, None] * 2.0 / (e_cond[None, :] - e_pick[:, None])
    weighted = (moved[:, :WIN].astype(jnp.float32) * weight.reshape(count, 1)).astype(jnp.bfloat16)
    return (moved, weighted)

def reference(cond_orbitals, cond_energy, val_orbitals, val_energy, val_slots, owner_count):
    table_a = cosine_table(GA)
    table_b = cosine_table(GB)
    val_float = val_energy.astype(jnp.float32)

    def one_lane(lane):
        cond_all = cond_orbitals[lane].T.reshape(N_PAIR, BC, GA * GB)
        energy_all = cond_energy[lane].reshape(N_PAIR, BC)

        def add_owner(total, owner):
            slots = val_slots[lane, owner]
            picked = jnp.take(val_orbitals, slots, axis=0)
            e_pick = jnp.take(val_float, slots)
            live = (lax.iota(jnp.int32, SLOTS) < owner_count[lane, owner]).astype(jnp.float32)
            moved, weighted = owner_terms(picked, e_pick, live, cond_all[owner], energy_all[owner], table_a, table_b)
            term = lax.dot_general(moved.astype(jnp.float32), weighted.astype(jnp.float32), (((0,), (0,)), ((), ())))
            return (total + term, None)
        start = jnp.zeros((GA * GB, WIN), jnp.float32)
        total, unused = lax.scan(add_owner, start, jnp.arange(N_PAIR, dtype=jnp.int32))
        return total * (2.0 / (SLOTS * BC * N_PAIR))
    return lax.map(one_lane, jnp.arange(LANES, dtype=jnp.int32))
```

```python
import jax
import jax.numpy as jnp
from jax import lax
from jax.experimental import pallas as pl
from jax.experimental.pallas import tpu as pltpu
from jax.sharding import PartitionSpec as P

BC = 128
GA = 16
GB = 128
WIN = 512
SLOTS = 16
GRID = 2048
NC = 8192
N_KA = 8
N_PAIR = 64
OWN = GRID // N_PAIR
PAIRS = SLOTS * BC
BLOCK = OWN + GA + 8

f32 = jnp.float32
bf16 = jnp.bfloat16


def cosine_table(length):
    freq = lax.iota(jnp.float32, length)[:, None]
    point = lax.iota(jnp.float32, length)[None, :]
    factor = jnp.where(freq == 0, jnp.sqrt(1.0 / length), jnp.sqrt(2.0 / length))
    return (factor * jnp.cos(jnp.pi * (point + 0.5) * freq / length)).astype(jnp.bfloat16)


def vmem(count):
    return [pl.BlockSpec(memory_space=pltpu.VMEM)] * count


def params():
    return pltpu.CompilerParams(vmem_limit_bytes=48 * 2**20)


def pack_kernel(cond_ref, val_ref, energy_ref, out_ref):
    for d in range(N_PAIR):
        out_ref[d, :OWN, :] = cond_ref[:, d * BC:(d + 1) * BC]
        out_ref[d, OWN:OWN + GA, :] = val_ref[...]
        out_ref[d, OWN + GA:, :] = energy_ref[...]


def pick_kernel(base_ref, slots_ref, got_ref, out_ref, cond_ref):
    base = base_ref[0]
    row = lax.broadcasted_iota(jnp.int32, (SLOTS, GB), 0)
    for k in range(N_KA):
        energies = jnp.zeros((SLOTS, GB), f32)
        for s in range(SLOTS):
            local = slots_ref[k, s] - base
            mine = jnp.logical_and(local >= 0, local < N_PAIR)
            local = jnp.clip(local, 0, N_PAIR - 1)
            keep = jnp.where(mine, 1.0, 0.0).astype(f32)
            orbital = got_ref[local, OWN:OWN + GA, :].astype(f32)
            out_ref[k, s] = (orbital * keep).astype(bf16)
            level = got_ref[local, OWN + GA:, :].astype(f32)[:1] * keep
            energies = jnp.where(row == s, level, energies)
        out_ref[k, SLOTS] = energies.astype(bf16)
    for d in range(N_PAIR):
        cond_ref[d] = got_ref[d, :OWN, :]


def owner_kernel(count_ref, cond_ref, pick_ref, e_pick_ref, e_cond_ref, bd_ref, ta_ref, out_ref,
                 pair_s, first_s, moved_s, wtd_s, weight_s):
    live = lax.broadcasted_iota(jnp.int32, (SLOTS, BC), 0) < count_ref[0]
    weight_s[...] = jnp.where(live, 1.0, 0.0) * 2.0 / (e_cond_ref[...] - e_pick_ref[...])

    def to_first(i, carry):
        start = pl.multiple_of(i * 256, 256)
        cond = cond_ref[pl.ds(start, 256), :].astype(f32)
        pick = pick_ref[pl.ds(start, 256), :]
        for s in range(SLOTS):
            pair_s[:, s * BC:(s + 1) * BC] = (cond * pick[:, s:s + 1]).astype(bf16)
        first = jnp.dot(bd_ref[...], pair_s[...], preferred_element_type=f32).astype(bf16)
        for h in range(2):
            for kg in range(8):
                at = pl.multiple_of(kg * 256 + (2 * i + h) * 16, 16)
                first_s[pl.ds(at, 16), :] = first[h * 128 + kg * 16:h * 128 + kg * 16 + 16, :]
        return carry

    lax.fori_loop(0, 8, to_first, 0)

    def to_moved(kg, carry):
        start = pl.multiple_of(kg * 256, 256)
        moved = jnp.dot(ta_ref[...], first_s[pl.ds(start, 256), :], preferred_element_type=f32)
        moved = moved.astype(bf16)
        for j in range(GA):
            at = pl.multiple_of(j * GB + kg * 16, 16)
            rows = moved[j * 16:j * 16 + 16, :]
            moved_s[pl.ds(at, 16), :] = rows
            if j < WIN // GB:
                for s in range(SLOTS):
                    part = rows[:, s * BC:(s + 1) * BC].astype(f32) * weight_s[s:s + 1, :]
                    wtd_s[pl.ds(at, 16), s * BC:(s + 1) * BC] = part.astype(bf16)
        return carry

    lax.fori_loop(0, 8, to_moved, 0)

    def to_out(i, carry):
        start = pl.multiple_of(i * 256, 256)
        total = lax.dot_general(
            moved_s[pl.ds(start, 256), :], wtd_s[...], (((1,), (1,)), ((), ())),
            preferred_element_type=f32,
        )
        out_ref[pl.ds(start, 256), :] = (total * (2.0 / (SLOTS * BC * N_PAIR))).astype(bf16)
        return carry

    lax.fori_loop(0, 8, to_out, 0)


def shards(cond_orbitals, cond_energy, val_orbitals, val_energy, val_slots, owner_count):
    slots = lax.all_gather(val_slots[0], "ka", axis=0, tiled=True)
    base = (lax.axis_index("ka") * N_PAIR).astype(jnp.int32).reshape(1)

    packed = pl.pallas_call(
        pack_kernel,
        out_shape=jax.ShapeDtypeStruct((N_PAIR, BLOCK, BC), bf16),
        in_specs=vmem(3),
        out_specs=vmem(1)[0],
        compiler_params=params(),
        name="pack",
    )(cond_orbitals[0], val_orbitals.reshape(GA, GB), jnp.broadcast_to(val_energy[:, None], (8, GB)))
    got = lax.all_to_all(packed, "pair", 0, 0, tiled=True)

    routed, cond = pl.pallas_call(
        pick_kernel,
        out_shape=(
            jax.ShapeDtypeStruct((N_KA, SLOTS + 1, GA, GB), bf16),
            jax.ShapeDtypeStruct((N_PAIR, OWN, BC), bf16),
        ),
        in_specs=[pl.BlockSpec(memory_space=pltpu.SMEM)] * 2 + vmem(1),
        out_specs=tuple(vmem(2)),
        compiler_params=params(),
        name="pick",
    )(base, slots, got)
    routed = lax.all_to_all(routed, "ka", 0, 0, tiled=True)
    merged = jnp.sum(routed.astype(f32), axis=0)
    picked = merged[:SLOTS].reshape(SLOTS, GRID).T
    e_pick = merged[SLOTS]

    bd = jnp.kron(jnp.eye(2, dtype=f32), cosine_table(GB).astype(f32)).astype(bf16)
    ta = jnp.kron(cosine_table(GA).astype(f32), jnp.eye(16, dtype=f32)).astype(bf16)
    part = pl.pallas_call(
        owner_kernel,
        out_shape=jax.ShapeDtypeStruct((GRID, WIN), bf16),
        in_specs=[pl.BlockSpec(memory_space=pltpu.SMEM)] + vmem(6),
        out_specs=vmem(1)[0],
        scratch_shapes=[
            pltpu.VMEM((256, PAIRS), bf16),
            pltpu.VMEM((GRID, PAIRS), bf16),
            pltpu.VMEM((GRID, PAIRS), bf16),
            pltpu.VMEM((WIN, PAIRS), bf16),
            pltpu.VMEM((SLOTS, BC), f32),
        ],
        compiler_params=params(),
        name="owner",
    )(owner_count[0], cond.reshape(GRID, BC), picked, e_pick, cond_energy, bd, ta)

    parts = lax.all_to_all(part.reshape(N_PAIR, OWN, WIN), "pair", 0, 0, tiled=True)
    return jnp.sum(parts.astype(f32), axis=0)[None]


def solution(mesh):
    return jax.shard_map(
        shards,
        mesh=mesh,
        in_specs=(
            P("ka", "pair", None),
            P("ka", "pair"),
            P(("ka", "pair"), None),
            P(("ka", "pair")),
            P("ka", "pair", None),
            P("ka", "pair"),
        ),
        out_specs=P("ka", "pair", None),
        check_vma=False,
    )
```

```python
import jax
import jax.numpy as jnp
from jax import lax
from jax.experimental import pallas as pl
from jax.experimental.pallas import tpu as pltpu
from jax.sharding import Mesh, PartitionSpec as P

BC = 128
GA = 16
GB = 128
WIN = 512
SLOTS = 16
GRID = 2048
NC = 8192
N_KA = 8
N_PAIR = 64
N_Y = 8
N_ZH = 2
N_X = 4
OWN = GRID // N_PAIR
COLS_X = 384
PAIRS = SLOTS * BC
BLOCK = OWN + GA + 8

PAIR = ("y", "zh", "x")

f32 = jnp.float32
bf16 = jnp.bfloat16


def cosine_table(length):
    freq = lax.iota(jnp.float32, length)[:, None]
    point = lax.iota(jnp.float32, length)[None, :]
    factor = jnp.where(freq == 0, jnp.sqrt(1.0 / length), jnp.sqrt(2.0 / length))
    return (factor * jnp.cos(jnp.pi * (point + 0.5) * freq / length)).astype(jnp.bfloat16)


def vmem(count):
    return [pl.BlockSpec(memory_space=pltpu.VMEM)] * count


def params():
    return pltpu.CompilerParams(vmem_limit_bytes=48 * 2**20)


def pack_kernel(cond_ref, val_ref, energy_ref, out_ref):
    for d in range(N_PAIR):
        out_ref[d, :OWN, :] = cond_ref[:, d * BC:(d + 1) * BC]
        out_ref[d, OWN:OWN + GA, :] = val_ref[...]
        out_ref[d, OWN + GA:, :] = energy_ref[...]


def pick_kernel(base_ref, slots_ref, got_ref, out_ref, cond_ref):
    base = base_ref[0]
    row = lax.broadcasted_iota(jnp.int32, (SLOTS, GB), 0)
    for k in range(N_KA):
        energies = jnp.zeros((SLOTS, GB), f32)
        for s in range(SLOTS):
            local = slots_ref[k, s] - base
            mine = jnp.logical_and(local >= 0, local < N_PAIR)
            local = jnp.clip(local, 0, N_PAIR - 1)
            keep = jnp.where(mine, 1.0, 0.0).astype(f32)
            orbital = got_ref[local, OWN:OWN + GA, :].astype(f32)
            out_ref[k, s] = (orbital * keep).astype(bf16)
            level = got_ref[local, OWN + GA:, :].astype(f32)[:1] * keep
            energies = jnp.where(row == s, level, energies)
        out_ref[k, SLOTS] = energies.astype(bf16)
    for d in range(N_PAIR):
        cond_ref[d] = got_ref[d, :OWN, :]


def owner_kernel(count_ref, cond_ref, pick_ref, e_pick_ref, e_cond_ref, bd_ref, ta_ref, x_ref, y_ref,
                 pair_s, first_s, moved_s, wtd_s, weight_s):
    live = lax.broadcasted_iota(jnp.int32, (SLOTS, BC), 0) < count_ref[0]
    weight_s[...] = jnp.where(live, 1.0, 0.0) * 2.0 / (e_cond_ref[...] - e_pick_ref[...])

    def to_first(i, carry):
        start = pl.multiple_of(i * 256, 256)
        cond = cond_ref[pl.ds(start, 256), :].astype(f32)
        pick = pick_ref[pl.ds(start, 256), :]
        for s in range(SLOTS):
            pair_s[:, s * BC:(s + 1) * BC] = (cond * pick[:, s:s + 1]).astype(bf16)
        first = jnp.dot(bd_ref[...], pair_s[...], preferred_element_type=f32).astype(bf16)
        for h in range(2):
            for kg in range(8):
                at = pl.multiple_of(kg * 256 + (2 * i + h) * 16, 16)
                first_s[pl.ds(at, 16), :] = first[h * 128 + kg * 16:h * 128 + kg * 16 + 16, :]
        return carry

    lax.fori_loop(0, 8, to_first, 0)

    def to_moved(kg, carry):
        start = pl.multiple_of(kg * 256, 256)
        moved = jnp.dot(ta_ref[...], first_s[pl.ds(start, 256), :], preferred_element_type=f32)
        moved = moved.astype(bf16)
        for j in range(GA):
            at = pl.multiple_of(j * GB + kg * 16, 16)
            rows = moved[j * 16:j * 16 + 16, :]
            moved_s[pl.ds(at, 16), :] = rows
            if j < WIN // GB:
                for s in range(SLOTS):
                    part = rows[:, s * BC:(s + 1) * BC].astype(f32) * weight_s[s:s + 1, :]
                    wtd_s[pl.ds(at, 16), s * BC:(s + 1) * BC] = part.astype(bf16)
        return carry

    lax.fori_loop(0, 8, to_moved, 0)

    def to_out(i, carry):
        start = pl.multiple_of(i * 256, 256)
        total = lax.dot_general(
            moved_s[pl.ds(start, 256), :], wtd_s[...], (((1,), (1,)), ((), ())),
            preferred_element_type=f32,
        )
        total = (total * (2.0 / (SLOTS * BC * N_PAIR))).astype(bf16)
        for t in range(8):
            rows = total[t * OWN:(t + 1) * OWN]
            x_ref[t % N_X, 2 * i + t // N_X] = rows[:, :COLS_X]
            y_ref[i, t] = rows[:, COLS_X:]
        return carry

    lax.fori_loop(0, 8, to_out, 0)


def shards(cond_orbitals, cond_energy, val_orbitals, val_energy, val_slots, owner_count):
    slots = lax.all_gather(val_slots[0], "ka", axis=0, tiled=True)
    base = (lax.axis_index("ka") * N_PAIR).astype(jnp.int32).reshape(1)

    packed = pl.pallas_call(
        pack_kernel,
        out_shape=jax.ShapeDtypeStruct((N_PAIR, BLOCK, BC), bf16),
        in_specs=vmem(3),
        out_specs=vmem(1)[0],
        compiler_params=params(),
        name="pack",
    )(cond_orbitals[0], val_orbitals.reshape(GA, GB), jnp.broadcast_to(val_energy[:, None], (8, GB)))
    got = lax.all_to_all(packed, PAIR, 0, 0, tiled=True)

    routed, cond = pl.pallas_call(
        pick_kernel,
        out_shape=(
            jax.ShapeDtypeStruct((N_KA, SLOTS + 1, GA, GB), bf16),
            jax.ShapeDtypeStruct((N_PAIR, OWN, BC), bf16),
        ),
        in_specs=[pl.BlockSpec(memory_space=pltpu.SMEM)] * 2 + vmem(1),
        out_specs=tuple(vmem(2)),
        compiler_params=params(),
        name="pick",
    )(base, slots, got)
    routed = lax.all_to_all(routed, "ka", 0, 0, tiled=True)
    merged = jnp.sum(routed.astype(f32), axis=0)
    picked = merged[:SLOTS].reshape(SLOTS, GRID).T
    e_pick = merged[SLOTS]

    bd = jnp.kron(jnp.eye(2, dtype=f32), cosine_table(GB).astype(f32)).astype(bf16)
    ta = jnp.kron(cosine_table(GA).astype(f32), jnp.eye(16, dtype=f32)).astype(bf16)
    part_x, part_y = pl.pallas_call(
        owner_kernel,
        out_shape=(
            jax.ShapeDtypeStruct((N_X, N_Y * N_ZH, OWN, COLS_X), bf16),
            jax.ShapeDtypeStruct((N_Y, N_ZH * N_X, OWN, WIN - COLS_X), bf16),
        ),
        in_specs=[pl.BlockSpec(memory_space=pltpu.SMEM)] + vmem(6),
        out_specs=tuple(vmem(2)),
        scratch_shapes=[
            pltpu.VMEM((256, PAIRS), bf16),
            pltpu.VMEM((GRID, PAIRS), bf16),
            pltpu.VMEM((GRID, PAIRS), bf16),
            pltpu.VMEM((WIN, PAIRS), bf16),
            pltpu.VMEM((SLOTS, BC), f32),
        ],
        compiler_params=params(),
        name="owner",
    )(owner_count[0], cond.reshape(GRID, BC), picked, e_pick, cond_energy, bd, ta)

    part_x = lax.all_to_all(part_x, "x", 0, 0, tiled=True)
    part_y = lax.all_to_all(part_y, "y", 0, 0, tiled=True)
    part_x = jnp.sum(part_x.astype(f32), axis=0).astype(bf16)
    part_y = jnp.sum(part_y.astype(f32), axis=0).astype(bf16)
    part_x = lax.all_to_all(part_x, ("y", "zh"), 0, 0, tiled=True)
    part_y = lax.all_to_all(part_y, ("zh", "x"), 0, 0, tiled=True)
    part_x = jnp.sum(part_x.astype(f32), axis=0)
    part_y = jnp.sum(part_y.astype(f32), axis=0)
    return jnp.concatenate([part_x, part_y], axis=1)[None]


def solution(mesh):
    mesh = Mesh(mesh.devices.reshape(N_KA, N_Y, N_ZH, N_X), ("ka", "y", "zh", "x"))
    return jax.shard_map(
        shards,
        mesh=mesh,
        in_specs=(
            P("ka", PAIR, None),
            P("ka", PAIR),
            P(("ka",) + PAIR, None),
            P(("ka",) + PAIR),
            P("ka", PAIR, None),
            P("ka", PAIR),
        ),
        out_specs=P("ka", PAIR, None),
        check_vma=False,
    )
```

```python
import jax
import jax.numpy as jnp
from jax import lax
from jax.experimental import pallas as pl
from jax.experimental.pallas import tpu as pltpu
from jax.sharding import Mesh, PartitionSpec as P

BC = 128
GA = 16
GB = 128
WIN = 512
SLOTS = 16
GRID = 2048
NC = 8192
N_KA = 8
N_PAIR = 64
N_Y = 8
N_ZH = 2
N_X = 4
OWN = GRID // N_PAIR
PAIRS = SLOTS * BC
BLOCK = OWN + GA + 8

PAIR = ("y", "zh", "x")

f32 = jnp.float32
bf16 = jnp.bfloat16


def cosine_table(length):
    freq = lax.iota(jnp.float32, length)[:, None]
    point = lax.iota(jnp.float32, length)[None, :]
    factor = jnp.where(freq == 0, jnp.sqrt(1.0 / length), jnp.sqrt(2.0 / length))
    return (factor * jnp.cos(jnp.pi * (point + 0.5) * freq / length)).astype(jnp.bfloat16)


def vmem(count):
    return [pl.BlockSpec(memory_space=pltpu.VMEM)] * count


def params():
    return pltpu.CompilerParams(vmem_limit_bytes=48 * 2**20)


def pack_kernel(cond_ref, val_ref, energy_ref, out_ref):
    for d in range(N_PAIR):
        out_ref[d, :OWN, :] = cond_ref[:, d * BC:(d + 1) * BC]
        out_ref[d, OWN:OWN + GA, :] = val_ref[...]
        out_ref[d, OWN + GA:, :] = energy_ref[...]


def pick_kernel(base_ref, slots_ref, got_ref, out_ref, cond_ref):
    base = base_ref[0]
    row = lax.broadcasted_iota(jnp.int32, (SLOTS, GB), 0)
    for k in range(N_KA):
        energies = jnp.zeros((SLOTS, GB), f32)
        for s in range(SLOTS):
            local = slots_ref[k, s] - base
            mine = jnp.logical_and(local >= 0, local < N_PAIR)
            local = jnp.clip(local, 0, N_PAIR - 1)
            keep = jnp.where(mine, 1.0, 0.0).astype(f32)
            orbital = got_ref[local, OWN:OWN + GA, :].astype(f32)
            out_ref[k, s] = (orbital * keep).astype(bf16)
            level = got_ref[local, OWN + GA:, :].astype(f32)[:1] * keep
            energies = jnp.where(row == s, level, energies)
        out_ref[k, SLOTS] = energies.astype(bf16)
    for d in range(N_PAIR):
        cond_ref[d] = got_ref[d, :OWN, :]


def owner_kernel(count_ref, cond_ref, pick_ref, e_pick_ref, e_cond_ref, bd_ref, ta_ref, out_ref,
                 pair_s, first_s, moved_s, wtd_s, weight_s):
    live = lax.broadcasted_iota(jnp.int32, (SLOTS, BC), 0) < count_ref[0]
    weight_s[...] = jnp.where(live, 1.0, 0.0) * 2.0 / (e_cond_ref[...] - e_pick_ref[...])

    def to_first(i, carry):
        start = pl.multiple_of(i * 256, 256)
        cond = cond_ref[pl.ds(start, 256), :].astype(f32)
        pick = pick_ref[pl.ds(start, 256), :]
        for s in range(SLOTS):
            pair_s[:, s * BC:(s + 1) * BC] = (cond * pick[:, s:s + 1]).astype(bf16)
        first = jnp.dot(bd_ref[...], pair_s[...], preferred_element_type=f32).astype(bf16)
        for h in range(2):
            for kg in range(8):
                at = pl.multiple_of(kg * 256 + (2 * i + h) * 16, 16)
                first_s[pl.ds(at, 16), :] = first[h * 128 + kg * 16:h * 128 + kg * 16 + 16, :]
        return carry

    lax.fori_loop(0, 8, to_first, 0)

    def to_moved(kg, carry):
        start = pl.multiple_of(kg * 256, 256)
        moved = jnp.dot(ta_ref[...], first_s[pl.ds(start, 256), :], preferred_element_type=f32)
        moved = moved.astype(bf16)
        for j in range(GA):
            at = pl.multiple_of(j * GB + kg * 16, 16)
            rows = moved[j * 16:j * 16 + 16, :]
            moved_s[pl.ds(at, 16), :] = rows
            if j < WIN // GB:
                for s in range(SLOTS):
                    part = rows[:, s * BC:(s + 1) * BC].astype(f32) * weight_s[s:s + 1, :]
                    wtd_s[pl.ds(at, 16), s * BC:(s + 1) * BC] = part.astype(bf16)
        return carry

    lax.fori_loop(0, 8, to_moved, 0)

    def to_out(i, carry):
        start = pl.multiple_of(i * 256, 256)
        total = lax.dot_general(
            moved_s[pl.ds(start, 256), :], wtd_s[...], (((1,), (1,)), ((), ())),
            preferred_element_type=f32,
        )
        total = (total * (2.0 / (SLOTS * BC * N_PAIR))).astype(bf16)
        for t in range(8):
            out_ref[t % N_X, 2 * i + t // N_X] = total[t * OWN:(t + 1) * OWN]
        return carry

    lax.fori_loop(0, 8, to_out, 0)


def shards(cond_orbitals, cond_energy, val_orbitals, val_energy, val_slots, owner_count):
    slots = lax.all_gather(val_slots[0], "ka", axis=0, tiled=True)
    base = (lax.axis_index("ka") * N_PAIR).astype(jnp.int32).reshape(1)

    packed = pl.pallas_call(
        pack_kernel,
        out_shape=jax.ShapeDtypeStruct((N_PAIR, BLOCK, BC), bf16),
        in_specs=vmem(3),
        out_specs=vmem(1)[0],
        compiler_params=params(),
        name="pack",
    )(cond_orbitals[0], val_orbitals.reshape(GA, GB), jnp.broadcast_to(val_energy[:, None], (8, GB)))
    got = lax.all_to_all(packed, PAIR, 0, 0, tiled=True)

    routed, cond = pl.pallas_call(
        pick_kernel,
        out_shape=(
            jax.ShapeDtypeStruct((N_KA, SLOTS + 1, GA, GB), bf16),
            jax.ShapeDtypeStruct((N_PAIR, OWN, BC), bf16),
        ),
        in_specs=[pl.BlockSpec(memory_space=pltpu.SMEM)] * 2 + vmem(1),
        out_specs=tuple(vmem(2)),
        compiler_params=params(),
        name="pick",
    )(base, slots, got)
    routed = lax.all_to_all(routed, "ka", 0, 0, tiled=True)
    merged = jnp.sum(routed.astype(f32), axis=0)
    picked = merged[:SLOTS].reshape(SLOTS, GRID).T
    e_pick = merged[SLOTS]

    bd = jnp.kron(jnp.eye(2, dtype=f32), cosine_table(GB).astype(f32)).astype(bf16)
    ta = jnp.kron(cosine_table(GA).astype(f32), jnp.eye(16, dtype=f32)).astype(bf16)
    part = pl.pallas_call(
        owner_kernel,
        out_shape=jax.ShapeDtypeStruct((N_X, N_Y * N_ZH, OWN, WIN), bf16),
        in_specs=[pl.BlockSpec(memory_space=pltpu.SMEM)] + vmem(6),
        out_specs=vmem(1)[0],
        scratch_shapes=[
            pltpu.VMEM((256, PAIRS), bf16),
            pltpu.VMEM((GRID, PAIRS), bf16),
            pltpu.VMEM((GRID, PAIRS), bf16),
            pltpu.VMEM((WIN, PAIRS), bf16),
            pltpu.VMEM((SLOTS, BC), f32),
        ],
        compiler_params=params(),
        name="owner",
    )(owner_count[0], cond.reshape(GRID, BC), picked, e_pick, cond_energy, bd, ta)

    part = lax.all_to_all(part, "x", 0, 0, tiled=True)
    part = jnp.sum(part.astype(f32), axis=0).astype(bf16)
    part = lax.all_to_all(part, ("y", "zh"), 0, 0, tiled=True)
    return jnp.sum(part.astype(f32), axis=0)[None]


def solution(mesh):
    mesh = Mesh(mesh.devices.reshape(N_KA, N_Y, N_ZH, N_X), ("ka", "y", "zh", "x"))
    return jax.shard_map(
        shards,
        mesh=mesh,
        in_specs=(
            P("ka", PAIR, None),
            P("ka", PAIR),
            P(("ka",) + PAIR, None),
            P(("ka",) + PAIR),
            P("ka", PAIR, None),
            P("ka", PAIR),
        ),
        out_specs=P("ka", PAIR, None),
        check_vma=False,
    )
```

```python
import jax
import jax.numpy as jnp
from jax import lax
from jax.experimental import pallas as pl
from jax.experimental.pallas import tpu as pltpu
from jax.sharding import Mesh, PartitionSpec as P

BC = 128
GA = 16
GB = 128
WIN = 512
SLOTS = 16
GRID = 2048
NC = 8192
N_KA = 8
N_PAIR = 64
N_Y = 8
N_ZH = 2
N_X = 4
OWN = GRID // N_PAIR
PAIRS = SLOTS * BC
GROUP = 4
BLOCK = OWN + 2 * N_KA + N_KA
ENERGY = OWN + 2 * N_KA

PAIR = ("y", "zh", "x")

f32 = jnp.float32
bf16 = jnp.bfloat16


def cosine_table(length):
    freq = lax.iota(jnp.float32, length)[:, None]
    point = lax.iota(jnp.float32, length)[None, :]
    factor = jnp.where(freq == 0, jnp.sqrt(1.0 / length), jnp.sqrt(2.0 / length))
    return (factor * jnp.cos(jnp.pi * (point + 0.5) * freq / length)).astype(jnp.bfloat16)


def vmem(count):
    return [pl.BlockSpec(memory_space=pltpu.VMEM)] * count


def params():
    return pltpu.CompilerParams(vmem_limit_bytes=48 * 2**20)


def pack_kernel(cond_ref, pieces_ref, out_ref):
    points = jnp.concatenate([pieces_ref[k, :2, :] for k in range(N_KA)], axis=0).astype(bf16)
    levels = jnp.concatenate([pieces_ref[k, 2:3, :] for k in range(N_KA)], axis=0).astype(bf16)
    for d in range(N_PAIR):
        out_ref[d, :OWN, :] = cond_ref[:, d * BC:(d + 1) * BC]
        out_ref[d, OWN:ENERGY, :] = points
        out_ref[d, ENERGY:, :] = levels


def pick_kernel(slots_ref, got_ref, out_ref, rows_s, picked_s):
    for d in range(N_PAIR):
        rows_s[d] = got_ref[d, OWN:, :].astype(f32)
    for k in range(N_KA):
        for s in range(SLOTS):
            slot = slots_ref[k, s]
            owner = lax.rem(slot, N_PAIR)
            line = lax.div(slot, N_PAIR)
            for a in range(2):
                picked_s[k, a, s:s + 1, :] = rows_s[owner, pl.ds(2 * line + a, 1), :]
            picked_s[k, 2, s:s + 1, :] = rows_s[owner, pl.ds(2 * N_KA + line, 1), :]
    out_ref[...] = picked_s[...].astype(bf16)


def owner_kernel(count_ref, got_ref, pick_ref, e_cond_ref, bd_ref, ta_ref, out_ref,
                 first_s, moved_s, wtd_s, weight_s):
    live = lax.broadcasted_iota(jnp.int32, (SLOTS, BC), 0) < count_ref[0]
    e_pick = pick_ref[0, 2].astype(f32)
    weight_s[...] = jnp.where(live, 1.0, 0.0) * 2.0 / (e_cond_ref[...] - e_pick)

    def to_first(i, carry):
        cond = [got_ref[8 * i + t, :OWN, :].astype(f32) for t in range(8)]
        cond = [jnp.concatenate(cond[4 * h:4 * h + 4], axis=0) for h in range(2)]
        pick = [pick_ref[i, h].astype(f32).T for h in range(2)]
        for s0 in range(0, SLOTS, GROUP):
            pair = [
                jnp.concatenate([cond[h] * pick[h][:, s:s + 1] for h in range(2)], axis=0).astype(bf16)
                for s in range(s0, s0 + GROUP)
            ]
            pair = jnp.concatenate(pair, axis=1)
            first = jnp.dot(bd_ref[...], pair, preferred_element_type=f32).astype(bf16)
            for h in range(2):
                for kg in range(8):
                    at = pl.multiple_of(kg * 256 + (2 * i + h) * 16, 16)
                    row = h * GB + kg * 16
                    first_s[pl.ds(at, 16), s0 * BC:(s0 + GROUP) * BC] = first[row:row + 16, :]
        return carry

    lax.fori_loop(0, 8, to_first, 0, unroll=4)

    def to_moved(kg, carry):
        start = pl.multiple_of(kg * 256, 256)
        for s0 in range(0, SLOTS, GROUP):
            lanes = slice(s0 * BC, (s0 + GROUP) * BC)
            moved = jnp.dot(ta_ref[...], first_s[pl.ds(start, 256), lanes], preferred_element_type=f32)
            moved = moved.astype(bf16)
            for j in range(GA):
                at = pl.multiple_of(j * GB + kg * 16, 16)
                rows = moved[j * 16:j * 16 + 16, :]
                moved_s[pl.ds(at, 16), lanes] = rows
                if j < WIN // GB:
                    for t in range(GROUP):
                        s = s0 + t
                        part = rows[:, t * BC:(t + 1) * BC].astype(f32) * weight_s[s:s + 1, :]
                        wtd_s[pl.ds(at, 16), s * BC:(s + 1) * BC] = part.astype(bf16)
        return carry

    lax.fori_loop(0, 8, to_moved, 0, unroll=4)

    def to_out(i, carry):
        start = pl.multiple_of(i * 256, 256)
        total = lax.dot_general(
            moved_s[pl.ds(start, 256), :], wtd_s[...], (((1,), (1,)), ((), ())),
            preferred_element_type=f32,
        )
        total = (total * (2.0 / (SLOTS * BC * N_PAIR))).astype(bf16)
        for t in range(8):
            out_ref[t % N_X, 2 * i + t // N_X] = total[t * OWN:(t + 1) * OWN]
        return carry

    lax.fori_loop(0, 8, to_out, 0, unroll=4)


def shards(cond_orbitals, cond_energy, val_orbitals, val_energy, val_slots, owner_count):
    points = val_orbitals.reshape(N_KA, 2, GB).astype(f32)
    level = jnp.broadcast_to(val_energy.astype(f32)[:, None, None], (N_KA, 1, GB))
    wanted = jnp.pad(val_slots[0].astype(f32), ((0, 0), (0, GB - SLOTS)))
    wanted = jnp.broadcast_to(wanted[None], (N_KA, 5, GB))
    pieces = lax.all_to_all(jnp.concatenate([points, level, wanted], axis=1), "ka", 0, 0, tiled=True)
    slots = pieces[:, 3, :SLOTS].astype(jnp.int32)

    packed = pl.pallas_call(
        pack_kernel,
        out_shape=jax.ShapeDtypeStruct((N_PAIR, BLOCK, BC), bf16),
        in_specs=vmem(2),
        out_specs=vmem(1)[0],
        compiler_params=params(),
        name="pack",
    )(cond_orbitals[0], pieces)
    got = lax.all_to_all(packed, PAIR, 0, 0, tiled=True)

    picked = pl.pallas_call(
        pick_kernel,
        out_shape=jax.ShapeDtypeStruct((N_KA, 3, SLOTS, GB), bf16),
        in_specs=[pl.BlockSpec(memory_space=pltpu.SMEM)] + vmem(1),
        out_specs=vmem(1)[0],
        scratch_shapes=[
            pltpu.VMEM((N_PAIR, BLOCK - OWN, GB), f32),
            pltpu.VMEM((N_KA, 3, SLOTS, GB), f32),
        ],
        compiler_params=params(),
        name="pick",
    )(slots, got)
    picked = lax.all_to_all(picked, "ka", 0, 0, tiled=True)

    bd = jnp.kron(jnp.eye(2, dtype=f32), cosine_table(GB).astype(f32)).astype(bf16)
    ta = jnp.kron(cosine_table(GA).astype(f32), jnp.eye(16, dtype=f32)).astype(bf16)
    part = pl.pallas_call(
        owner_kernel,
        out_shape=jax.ShapeDtypeStruct((N_X, N_Y * N_ZH, OWN, WIN), bf16),
        in_specs=[pl.BlockSpec(memory_space=pltpu.SMEM)] + vmem(5),
        out_specs=vmem(1)[0],
        scratch_shapes=[
            pltpu.VMEM((GRID, PAIRS), bf16),
            pltpu.VMEM((GRID, PAIRS), bf16),
            pltpu.VMEM((WIN, PAIRS), bf16),
            pltpu.VMEM((SLOTS, BC), f32),
        ],
        compiler_params=params(),
        name="owner",
    )(owner_count[0], got, picked, cond_energy, bd, ta)

    part = lax.all_to_all(part, "x", 0, 0, tiled=True)
    part = jnp.sum(part.astype(f32), axis=0).astype(bf16)
    part = lax.all_to_all(part, ("y", "zh"), 0, 0, tiled=True)
    return jnp.sum(part.astype(f32), axis=0)[None]


def solution(mesh):
    mesh = Mesh(mesh.devices.reshape(N_KA, N_Y, N_ZH, N_X), ("ka", "y", "zh", "x"))
    return jax.shard_map(
        shards,
        mesh=mesh,
        in_specs=(
            P("ka", PAIR, None),
            P("ka", PAIR),
            P(("ka",) + PAIR, None),
            P(("ka",) + PAIR),
            P("ka", PAIR, None),
            P("ka", PAIR),
        ),
        out_specs=P("ka", PAIR, None),
        check_vma=False,
    )
```

```python
import jax
import jax.numpy as jnp
from jax import lax
from jax.experimental import pallas as pl
from jax.experimental.pallas import tpu as pltpu
from jax.sharding import Mesh, PartitionSpec as P

BC = 128
GA = 16
GB = 128
WIN = 512
SLOTS = 16
GRID = 2048
NC = 8192
N_KA = 8
N_PAIR = 64
N_YH = 4
N_YL = 2
N_ZH = 2
N_X = 4
OWN = GRID // N_PAIR
PAIRS = SLOTS * BC
GROUP = 4
BLOCK = OWN + 2 * N_KA + N_KA
ENERGY = OWN + 2 * N_KA

PAIR = ("yh", "yl", "zh", "x")
NEAR = ("yl", "x")
FAR = ("yh", "zh")

f32 = jnp.float32
bf16 = jnp.bfloat16


def cosine_table(length):
    freq = lax.iota(jnp.float32, length)[:, None]
    point = lax.iota(jnp.float32, length)[None, :]
    factor = jnp.where(freq == 0, jnp.sqrt(1.0 / length), jnp.sqrt(2.0 / length))
    return (factor * jnp.cos(jnp.pi * (point + 0.5) * freq / length)).astype(jnp.bfloat16)


def vmem(count):
    return [pl.BlockSpec(memory_space=pltpu.VMEM)] * count


def params():
    return pltpu.CompilerParams(vmem_limit_bytes=48 * 2**20)


def pack_kernel(cond_ref, pieces_ref, out_ref):
    points = jnp.concatenate([pieces_ref[k, :2, :] for k in range(N_KA)], axis=0).astype(bf16)
    levels = jnp.concatenate([pieces_ref[k, 2:3, :] for k in range(N_KA)], axis=0).astype(bf16)
    for d in range(N_PAIR):
        out_ref[d, :OWN, :] = cond_ref[:, d * BC:(d + 1) * BC]
        out_ref[d, OWN:ENERGY, :] = points
        out_ref[d, ENERGY:, :] = levels


def pick_kernel(slots_ref, got_ref, out_ref, rows_s, picked_s):
    for d in range(N_PAIR):
        rows_s[d] = got_ref[d, OWN:, :].astype(f32)
    for k in range(N_KA):
        for s in range(SLOTS):
            slot = slots_ref[k, s]
            owner = lax.rem(slot, N_PAIR)
            line = lax.div(slot, N_PAIR)
            for a in range(2):
                picked_s[k, a, s:s + 1, :] = rows_s[owner, pl.ds(2 * line + a, 1), :]
            picked_s[k, 2, s:s + 1, :] = rows_s[owner, pl.ds(2 * N_KA + line, 1), :]
    out_ref[...] = picked_s[...].astype(bf16)


def owner_kernel(count_ref, got_ref, pick_ref, e_cond_ref, bd_ref, ta_ref, out_ref,
                 first_s, moved_s, wtd_s, weight_s):
    live = lax.broadcasted_iota(jnp.int32, (SLOTS, BC), 0) < count_ref[0]
    e_pick = pick_ref[0, 2].astype(f32)
    weight_s[...] = jnp.where(live, 1.0, 0.0) * 2.0 / (e_cond_ref[...] - e_pick)

    def to_first(i, carry):
        cond = [got_ref[8 * i + t, :OWN, :].astype(f32) for t in range(8)]
        cond = [jnp.concatenate(cond[4 * h:4 * h + 4], axis=0) for h in range(2)]
        pick = [pick_ref[i, h].astype(f32).T for h in range(2)]
        for s0 in range(0, SLOTS, GROUP):
            pair = [
                jnp.concatenate([cond[h] * pick[h][:, s:s + 1] for h in range(2)], axis=0).astype(bf16)
                for s in range(s0, s0 + GROUP)
            ]
            pair = jnp.concatenate(pair, axis=1)
            first = jnp.dot(bd_ref[...], pair, preferred_element_type=f32).astype(bf16)
            for h in range(2):
                for kg in range(8):
                    at = pl.multiple_of(kg * 256 + (2 * i + h) * 16, 16)
                    row = h * GB + kg * 16
                    first_s[pl.ds(at, 16), s0 * BC:(s0 + GROUP) * BC] = first[row:row + 16, :]
        return carry

    lax.fori_loop(0, 8, to_first, 0, unroll=4)

    def to_moved(kg, carry):
        start = pl.multiple_of(kg * 256, 256)
        for s0 in range(0, SLOTS, GROUP):
            lanes = slice(s0 * BC, (s0 + GROUP) * BC)
            moved = jnp.dot(ta_ref[...], first_s[pl.ds(start, 256), lanes], preferred_element_type=f32)
            moved = moved.astype(bf16)
            for j in range(GA):
                at = pl.multiple_of(j * GB + kg * 16, 16)
                rows = moved[j * 16:j * 16 + 16, :]
                moved_s[pl.ds(at, 16), lanes] = rows
                if j < WIN // GB:
                    for t in range(GROUP):
                        s = s0 + t
                        part = rows[:, t * BC:(t + 1) * BC].astype(f32) * weight_s[s:s + 1, :]
                        wtd_s[pl.ds(at, 16), s * BC:(s + 1) * BC] = part.astype(bf16)
        return carry

    lax.fori_loop(0, 8, to_moved, 0, unroll=4)

    def to_out(i, carry):
        start = pl.multiple_of(i * 256, 256)
        total = lax.dot_general(
            moved_s[pl.ds(start, 256), :], wtd_s[...], (((1,), (1,)), ((), ())),
            preferred_element_type=f32,
        )
        total = (total * (2.0 / (SLOTS * BC * N_PAIR))).astype(bf16)
        for t in range(8):
            near = lax.rem(i, N_YL) * N_X + t % N_X
            far = lax.div(i, N_YL) * N_ZH + t // N_X
            out_ref[near, far] = total[t * OWN:(t + 1) * OWN]
        return carry

    lax.fori_loop(0, 8, to_out, 0, unroll=4)


def shards(cond_orbitals, cond_energy, val_orbitals, val_energy, val_slots, owner_count):
    points = val_orbitals.reshape(N_KA, 2, GB).astype(f32)
    level = jnp.broadcast_to(val_energy.astype(f32)[:, None, None], (N_KA, 1, GB))
    wanted = jnp.pad(val_slots[0].astype(f32), ((0, 0), (0, GB - SLOTS)))
    wanted = jnp.broadcast_to(wanted[None], (N_KA, 5, GB))
    pieces = lax.all_to_all(jnp.concatenate([points, level, wanted], axis=1), "ka", 0, 0, tiled=True)
    slots = pieces[:, 3, :SLOTS].astype(jnp.int32)

    packed = pl.pallas_call(
        pack_kernel,
        out_shape=jax.ShapeDtypeStruct((N_PAIR, BLOCK, BC), bf16),
        in_specs=vmem(2),
        out_specs=vmem(1)[0],
        compiler_params=params(),
        name="pack",
    )(cond_orbitals[0], pieces)
    got = lax.all_to_all(packed, PAIR, 0, 0, tiled=True)

    picked = pl.pallas_call(
        pick_kernel,
        out_shape=jax.ShapeDtypeStruct((N_KA, 3, SLOTS, GB), bf16),
        in_specs=[pl.BlockSpec(memory_space=pltpu.SMEM)] + vmem(1),
        out_specs=vmem(1)[0],
        scratch_shapes=[
            pltpu.VMEM((N_PAIR, BLOCK - OWN, GB), f32),
            pltpu.VMEM((N_KA, 3, SLOTS, GB), f32),
        ],
        compiler_params=params(),
        name="pick",
    )(slots, got)
    picked = lax.all_to_all(picked, "ka", 0, 0, tiled=True)

    bd = jnp.kron(jnp.eye(2, dtype=f32), cosine_table(GB).astype(f32)).astype(bf16)
    ta = jnp.kron(cosine_table(GA).astype(f32), jnp.eye(16, dtype=f32)).astype(bf16)
    part = pl.pallas_call(
        owner_kernel,
        out_shape=jax.ShapeDtypeStruct((N_YL * N_X, N_YH * N_ZH, OWN, WIN), bf16),
        in_specs=[pl.BlockSpec(memory_space=pltpu.SMEM)] + vmem(5),
        out_specs=vmem(1)[0],
        scratch_shapes=[
            pltpu.VMEM((GRID, PAIRS), bf16),
            pltpu.VMEM((GRID, PAIRS), bf16),
            pltpu.VMEM((WIN, PAIRS), bf16),
            pltpu.VMEM((SLOTS, BC), f32),
        ],
        compiler_params=params(),
        name="owner",
    )(owner_count[0], got, picked, cond_energy, bd, ta)

    part = lax.all_to_all(part, NEAR, 0, 0, tiled=True)
    part = jnp.sum(part.astype(f32), axis=0).astype(bf16)
    part = lax.all_to_all(part, FAR, 0, 0, tiled=True)
    return jnp.sum(part.astype(f32), axis=0)[None]


def solution(mesh):
    mesh = Mesh(mesh.devices.reshape(N_KA, N_YH, N_YL, N_ZH, N_X), ("ka",) + PAIR)
    return jax.shard_map(
        shards,
        mesh=mesh,
        in_specs=(
            P("ka", PAIR, None),
            P("ka", PAIR),
            P(("ka",) + PAIR, None),
            P(("ka",) + PAIR),
            P("ka", PAIR, None),
            P("ka", PAIR),
        ),
        out_specs=P("ka", PAIR, None),
        check_vma=False,
    )
```

```python
import jax
import jax.numpy as jnp
from jax import lax
from jax.experimental import pallas as pl
from jax.experimental.pallas import tpu as pltpu
from jax.sharding import Mesh, PartitionSpec as P

BC = 128
GA = 16
GB = 128
WIN = 512
SLOTS = 16
GRID = 2048
NC = 8192
N_KA = 8
N_PAIR = 64
N_YH = 4
N_YL = 2
N_ZH = 2
N_X = 4
OWN = GRID // N_PAIR
PAIRS = SLOTS * BC
GROUP = 4
BLOCK = OWN + 2 * N_KA + N_KA
ENERGY = OWN + 2 * N_KA

PAIR = ("yh", "yl", "zh", "x")
NEAR = ("yl", "x")
FAR = ("yh", "zh")

f32 = jnp.float32
bf16 = jnp.bfloat16


def cosine_table(length):
    freq = lax.iota(jnp.float32, length)[:, None]
    point = lax.iota(jnp.float32, length)[None, :]
    factor = jnp.where(freq == 0, jnp.sqrt(1.0 / length), jnp.sqrt(2.0 / length))
    return (factor * jnp.cos(jnp.pi * (point + 0.5) * freq / length)).astype(jnp.bfloat16)


def vmem(count):
    return [pl.BlockSpec(memory_space=pltpu.VMEM)] * count


def params():
    return pltpu.CompilerParams(vmem_limit_bytes=48 * 2**20)


def cond_kernel(cond_ref, out_ref):
    for d in range(N_PAIR):
        out_ref[d] = cond_ref[:, d * BC:(d + 1) * BC]


def pack_kernel(pieces_ref, cond_ref, out_ref):
    points = jnp.concatenate([pieces_ref[k, :2, :] for k in range(N_KA)], axis=0).astype(bf16)
    levels = jnp.concatenate([pieces_ref[k, 2:3, :] for k in range(N_KA)], axis=0).astype(bf16)
    for d in range(N_PAIR):
        out_ref[d, :OWN, :] = cond_ref[d]
        out_ref[d, OWN:ENERGY, :] = points
        out_ref[d, ENERGY:, :] = levels


def pick_kernel(slots_ref, got_ref, out_ref, rows_s, picked_s):
    for d in range(N_PAIR):
        rows_s[d] = got_ref[d, OWN:, :].astype(f32)
    for k in range(N_KA):
        for s in range(SLOTS):
            slot = slots_ref[k, s]
            owner = jnp.bitwise_and(slot, N_PAIR - 1)
            line = lax.shift_right_logical(slot, 6)
            for a in range(2):
                picked_s[k, a, s:s + 1, :] = rows_s[owner, pl.ds(2 * line + a, 1), :]
            picked_s[k, 2, s:s + 1, :] = rows_s[owner, pl.ds(2 * N_KA + line, 1), :]
    out_ref[...] = picked_s[...].astype(bf16)


def owner_kernel(count_ref, got_ref, pick_ref, e_cond_ref, bd_ref, ta_ref, out_ref,
                 first_s, moved_s, wtd_s, weight_s):
    live = lax.broadcasted_iota(jnp.int32, (SLOTS, BC), 0) < count_ref[0]
    e_pick = pick_ref[0, 2].astype(f32)
    weight_s[...] = jnp.where(live, 1.0, 0.0) * 2.0 / (e_cond_ref[...] - e_pick)

    def to_first(i, carry):
        cond = [got_ref[8 * i + t, :OWN, :].astype(f32) for t in range(8)]
        cond = [jnp.concatenate(cond[4 * h:4 * h + 4], axis=0) for h in range(2)]
        pick = [pick_ref[i, h].astype(f32).T for h in range(2)]
        for s0 in range(0, SLOTS, GROUP):
            pair = [
                jnp.concatenate([cond[h] * pick[h][:, s:s + 1] for h in range(2)], axis=0).astype(bf16)
                for s in range(s0, s0 + GROUP)
            ]
            pair = jnp.concatenate(pair, axis=1)
            first = jnp.dot(bd_ref[...], pair, preferred_element_type=f32).astype(bf16)
            for h in range(2):
                for kg in range(8):
                    at = pl.multiple_of(kg * 256 + (2 * i + h) * 16, 16)
                    row = h * GB + kg * 16
                    first_s[pl.ds(at, 16), s0 * BC:(s0 + GROUP) * BC] = first[row:row + 16, :]
        return carry

    lax.fori_loop(0, 8, to_first, 0, unroll=8)

    def to_moved(kg, carry):
        start = pl.multiple_of(kg * 256, 256)
        for s0 in range(0, SLOTS, GROUP):
            lanes = slice(s0 * BC, (s0 + GROUP) * BC)
            moved = jnp.dot(ta_ref[...], first_s[pl.ds(start, 256), lanes], preferred_element_type=f32)
            moved = moved.astype(bf16)
            for j in range(GA):
                at = pl.multiple_of(j * GB + kg * 16, 16)
                rows = moved[j * 16:j * 16 + 16, :]
                moved_s[pl.ds(at, 16), lanes] = rows
                if j < WIN // GB:
                    for t in range(GROUP):
                        s = s0 + t
                        part = rows[:, t * BC:(t + 1) * BC].astype(f32) * weight_s[s:s + 1, :]
                        wtd_s[pl.ds(at, 16), s * BC:(s + 1) * BC] = part.astype(bf16)
        return carry

    lax.fori_loop(0, 8, to_moved, 0, unroll=8)

    def to_out(i, carry):
        start = pl.multiple_of(i * 256, 256)
        total = lax.dot_general(
            moved_s[pl.ds(start, 256), :], wtd_s[...], (((1,), (1,)), ((), ())),
            preferred_element_type=f32,
        )
        total = (total * (2.0 / (SLOTS * BC * N_PAIR))).astype(bf16)
        for t in range(8):
            near = lax.rem(i, N_YL) * N_X + t % N_X
            far = lax.div(i, N_YL) * N_ZH + t // N_X
            out_ref[near, far] = total[t * OWN:(t + 1) * OWN]
        return carry

    lax.fori_loop(0, 8, to_out, 0, unroll=8)


def shards(cond_orbitals, cond_energy, val_orbitals, val_energy, val_slots, owner_count):
    points = val_orbitals.reshape(N_KA, 2, GB).astype(f32)
    level = jnp.broadcast_to(val_energy.astype(f32)[:, None, None], (N_KA, 1, GB))
    wanted = jnp.pad(val_slots[0].astype(f32), ((0, 0), (0, GB - SLOTS)))
    wanted = jnp.broadcast_to(wanted[None], (N_KA, 5, GB))
    pieces = lax.all_to_all(jnp.concatenate([points, level, wanted], axis=1), "ka", 0, 0, tiled=True)
    slots = pieces[:, 3, :SLOTS].astype(jnp.int32)

    cond = pl.pallas_call(
        cond_kernel,
        out_shape=jax.ShapeDtypeStruct((N_PAIR, OWN, BC), bf16),
        in_specs=vmem(1),
        out_specs=vmem(1)[0],
        compiler_params=params(),
        name="cond",
    )(cond_orbitals[0])
    packed = pl.pallas_call(
        pack_kernel,
        out_shape=jax.ShapeDtypeStruct((N_PAIR, BLOCK, BC), bf16),
        in_specs=vmem(2),
        out_specs=vmem(1)[0],
        compiler_params=params(),
        name="pack",
    )(pieces, cond)
    got = lax.all_to_all(packed, PAIR, 0, 0, tiled=True)

    picked = pl.pallas_call(
        pick_kernel,
        out_shape=jax.ShapeDtypeStruct((N_KA, 3, SLOTS, GB), bf16),
        in_specs=[pl.BlockSpec(memory_space=pltpu.SMEM)] + vmem(1),
        out_specs=vmem(1)[0],
        scratch_shapes=[
            pltpu.VMEM((N_PAIR, BLOCK - OWN, GB), f32),
            pltpu.VMEM((N_KA, 3, SLOTS, GB), f32),
        ],
        compiler_params=params(),
        name="pick",
    )(slots, got)
    picked = lax.all_to_all(picked, "ka", 0, 0, tiled=True)

    bd = jnp.kron(jnp.eye(2, dtype=f32), cosine_table(GB).astype(f32)).astype(bf16)
    ta = jnp.kron(cosine_table(GA).astype(f32), jnp.eye(16, dtype=f32)).astype(bf16)
    part = pl.pallas_call(
        owner_kernel,
        out_shape=jax.ShapeDtypeStruct((N_YL * N_X, N_YH * N_ZH, OWN, WIN), bf16),
        in_specs=[pl.BlockSpec(memory_space=pltpu.SMEM)] + vmem(5),
        out_specs=vmem(1)[0],
        scratch_shapes=[
            pltpu.VMEM((GRID, PAIRS), bf16),
            pltpu.VMEM((GRID, PAIRS), bf16),
            pltpu.VMEM((WIN, PAIRS), bf16),
            pltpu.VMEM((SLOTS, BC), f32),
        ],
        compiler_params=params(),
        name="owner",
    )(owner_count[0], got, picked, cond_energy, bd, ta)

    part = lax.all_to_all(part, NEAR, 0, 0, tiled=True)
    part = jnp.sum(part.astype(f32), axis=0).astype(bf16)
    part = lax.all_to_all(part, FAR, 0, 0, tiled=True)
    return jnp.sum(part.astype(f32), axis=0)[None]


def solution(mesh):
    mesh = Mesh(mesh.devices.reshape(N_KA, N_YH, N_YL, N_ZH, N_X), ("ka",) + PAIR)
    return jax.shard_map(
        shards,
        mesh=mesh,
        in_specs=(
            P("ka", PAIR, None),
            P("ka", PAIR),
            P(("ka",) + PAIR, None),
            P(("ka",) + PAIR),
            P("ka", PAIR, None),
            P("ka", PAIR),
        ),
        out_specs=P("ka", PAIR, None),
        check_vma=False,
    )
```

```python
import jax
import jax.numpy as jnp
from jax import lax
from jax.experimental import pallas as pl
from jax.experimental.pallas import tpu as pltpu
from jax.sharding import Mesh, PartitionSpec as P

BC = 128
GA = 16
GB = 128
WIN = 512
SLOTS = 16
GRID = 2048
NC = 8192
N_KA = 8
N_PAIR = 64
N_YH = 4
N_YL = 2
N_ZH = 2
N_X = 4
OWN = GRID // N_PAIR
PAIRS = SLOTS * BC
GROUP = 4
BLOCK = OWN + 2 * N_KA + N_KA
ENERGY = OWN + 2 * N_KA

PAIR = ("yh", "yl", "zh", "x")
NEAR = ("yl", "x")
FAR = ("yh", "zh")

f32 = jnp.float32
bf16 = jnp.bfloat16


def cosine_table(length):
    freq = lax.iota(jnp.float32, length)[:, None]
    point = lax.iota(jnp.float32, length)[None, :]
    factor = jnp.where(freq == 0, jnp.sqrt(1.0 / length), jnp.sqrt(2.0 / length))
    return (factor * jnp.cos(jnp.pi * (point + 0.5) * freq / length)).astype(jnp.bfloat16)


def vmem(count):
    return [pl.BlockSpec(memory_space=pltpu.VMEM)] * count


def params():
    return pltpu.CompilerParams(vmem_limit_bytes=48 * 2**20)


def piece_kernel(energy_ref, val_ref, slots_ref, out_ref, val_s, slots_s, sems):
    copies = [
        pltpu.make_async_copy(val_ref, val_s, sems.at[0]),
        pltpu.make_async_copy(slots_ref, slots_s, sems.at[1]),
    ]
    for copy in copies:
        copy.start()
    out_ref[...] = jnp.zeros_like(out_ref)
    for k in range(N_KA):
        out_ref[k, 2:3, :] = energy_ref[:1, :].astype(f32)
    for copy in copies:
        copy.wait()
    wanted = slots_s[...].astype(f32)
    for k in range(N_KA):
        for a in range(2):
            at = (2 * k + a) * GB
            out_ref[k, a:a + 1, :] = val_s[:, at:at + GB].astype(f32)
        out_ref[k, 3:4, :SLOTS] = wanted


def cond_kernel(cond_ref, out_ref):
    for d in range(N_PAIR):
        out_ref[d] = cond_ref[:, d * BC:(d + 1) * BC]


def pack_kernel(pieces_ref, cond_ref, out_ref):
    points = jnp.concatenate([pieces_ref[k, :2, :] for k in range(N_KA)], axis=0).astype(bf16)
    levels = jnp.concatenate([pieces_ref[k, 2:3, :] for k in range(N_KA)], axis=0).astype(bf16)
    for d in range(N_PAIR):
        out_ref[d, :OWN, :] = cond_ref[d]
        out_ref[d, OWN:ENERGY, :] = points
        out_ref[d, ENERGY:, :] = levels


def pick_kernel(slots_ref, got_ref, out_ref, rows_s, picked_s):
    for d in range(N_PAIR):
        rows_s[d] = got_ref[d, OWN:, :].astype(f32)
    for k in range(N_KA):
        for s in range(SLOTS):
            slot = slots_ref[k, s]
            owner = jnp.bitwise_and(slot, N_PAIR - 1)
            line = lax.shift_right_logical(slot, 6)
            for a in range(2):
                picked_s[k, a, s:s + 1, :] = rows_s[owner, pl.ds(2 * line + a, 1), :]
            picked_s[k, 2, s:s + 1, :] = rows_s[owner, pl.ds(2 * N_KA + line, 1), :]
    out_ref[...] = picked_s[...].astype(bf16)


def owner_kernel(count_ref, got_ref, pick_ref, e_cond_ref, bd_ref, ta_ref, out_ref,
                 first_s, moved_s, wtd_s, weight_s):
    live = lax.broadcasted_iota(jnp.int32, (SLOTS, BC), 0) < count_ref[0]
    e_pick = pick_ref[0, 2].astype(f32)
    weight_s[...] = jnp.where(live, 1.0, 0.0) * 2.0 / (e_cond_ref[...] - e_pick)

    def to_first(i, carry):
        cond = [got_ref[8 * i + t, :OWN, :].astype(f32) for t in range(8)]
        cond = [jnp.concatenate(cond[4 * h:4 * h + 4], axis=0) for h in range(2)]
        pick = [pick_ref[i, h].astype(f32).T for h in range(2)]
        for s0 in range(0, SLOTS, GROUP):
            pair = [
                jnp.concatenate([cond[h] * pick[h][:, s:s + 1] for h in range(2)], axis=0).astype(bf16)
                for s in range(s0, s0 + GROUP)
            ]
            pair = jnp.concatenate(pair, axis=1)
            first = jnp.dot(bd_ref[...], pair, preferred_element_type=f32).astype(bf16)
            for h in range(2):
                for kg in range(8):
                    at = pl.multiple_of(kg * 256 + (2 * i + h) * 16, 16)
                    row = h * GB + kg * 16
                    first_s[pl.ds(at, 16), s0 * BC:(s0 + GROUP) * BC] = first[row:row + 16, :]
        return carry

    lax.fori_loop(0, 8, to_first, 0, unroll=4)

    def to_moved(kg, carry):
        start = pl.multiple_of(kg * 256, 256)
        for s0 in range(0, SLOTS, GROUP):
            lanes = slice(s0 * BC, (s0 + GROUP) * BC)
            moved = jnp.dot(ta_ref[...], first_s[pl.ds(start, 256), lanes], preferred_element_type=f32)
            moved = moved.astype(bf16)
            for j in range(GA):
                at = pl.multiple_of(j * GB + kg * 16, 16)
                rows = moved[j * 16:j * 16 + 16, :]
                moved_s[pl.ds(at, 16), lanes] = rows
                if j < WIN // GB:
                    for t in range(GROUP):
                        s = s0 + t
                        part = rows[:, t * BC:(t + 1) * BC].astype(f32) * weight_s[s:s + 1, :]
                        wtd_s[pl.ds(at, 16), s * BC:(s + 1) * BC] = part.astype(bf16)
        return carry

    lax.fori_loop(0, 8, to_moved, 0, unroll=4)

    def to_out(i, carry):
        start = pl.multiple_of(i * 256, 256)
        total = lax.dot_general(
            moved_s[pl.ds(start, 256), :], wtd_s[...], (((1,), (1,)), ((), ())),
            preferred_element_type=f32,
        )
        total = (total * (2.0 / (SLOTS * BC * N_PAIR))).astype(bf16)
        for t in range(8):
            near = lax.rem(i, N_YL) * N_X + t % N_X
            far = lax.div(i, N_YL) * N_ZH + t // N_X
            out_ref[near, far] = total[t * OWN:(t + 1) * OWN]
        return carry

    lax.fori_loop(0, 8, to_out, 0, unroll=4)


def shards(cond_orbitals, cond_energy, val_orbitals, val_energy, val_slots, owner_count):
    pieces = pl.pallas_call(
        piece_kernel,
        out_shape=jax.ShapeDtypeStruct((N_KA, 8, GB), f32),
        in_specs=vmem(1) + [pl.BlockSpec(memory_space=pl.ANY)] * 2,
        out_specs=vmem(1)[0],
        scratch_shapes=[
            pltpu.VMEM((1, GRID), bf16),
            pltpu.VMEM((1, SLOTS), jnp.int32),
            pltpu.SemaphoreType.DMA((2,)),
        ],
        compiler_params=pltpu.CompilerParams(vmem_limit_bytes=60 * 2**20),
        name="piece",
    )(jnp.broadcast_to(val_energy[:, None], (8, GB)), val_orbitals, val_slots[0])
    pieces = lax.all_to_all(pieces, "ka", 0, 0, tiled=True)
    slots = pieces[:, 3, :SLOTS].astype(jnp.int32)

    cond = pl.pallas_call(
        cond_kernel,
        out_shape=jax.ShapeDtypeStruct((N_PAIR, OWN, BC), bf16),
        in_specs=vmem(1),
        out_specs=vmem(1)[0],
        compiler_params=params(),
        name="cond",
    )(cond_orbitals[0])
    packed = pl.pallas_call(
        pack_kernel,
        out_shape=jax.ShapeDtypeStruct((N_PAIR, BLOCK, BC), bf16),
        in_specs=vmem(2),
        out_specs=vmem(1)[0],
        compiler_params=params(),
        name="pack",
    )(pieces, cond)
    got = lax.all_to_all(packed, PAIR, 0, 0, tiled=True)

    picked = pl.pallas_call(
        pick_kernel,
        out_shape=jax.ShapeDtypeStruct((N_KA, 3, SLOTS, GB), bf16),
        in_specs=[pl.BlockSpec(memory_space=pltpu.SMEM)] + vmem(1),
        out_specs=vmem(1)[0],
        scratch_shapes=[
            pltpu.VMEM((N_PAIR, BLOCK - OWN, GB), f32),
            pltpu.VMEM((N_KA, 3, SLOTS, GB), f32),
        ],
        compiler_params=params(),
        name="pick",
    )(slots, got)
    picked = lax.all_to_all(picked, "ka", 0, 0, tiled=True)

    bd = jnp.kron(jnp.eye(2, dtype=f32), cosine_table(GB).astype(f32)).astype(bf16)
    ta = jnp.kron(cosine_table(GA).astype(f32), jnp.eye(16, dtype=f32)).astype(bf16)
    part = pl.pallas_call(
        owner_kernel,
        out_shape=jax.ShapeDtypeStruct((N_YL * N_X, N_YH * N_ZH, OWN, WIN), bf16),
        in_specs=[pl.BlockSpec(memory_space=pltpu.SMEM)] + vmem(5),
        out_specs=vmem(1)[0],
        scratch_shapes=[
            pltpu.VMEM((GRID, PAIRS), bf16),
            pltpu.VMEM((GRID, PAIRS), bf16),
            pltpu.VMEM((WIN, PAIRS), bf16),
            pltpu.VMEM((SLOTS, BC), f32),
        ],
        compiler_params=params(),
        name="owner",
    )(owner_count[0], got, picked, cond_energy, bd, ta)

    part = lax.all_to_all(part, NEAR, 0, 0, tiled=True)
    part = jnp.sum(part.astype(f32), axis=0).astype(bf16)
    part = lax.all_to_all(part, FAR, 0, 0, tiled=True)
    return jnp.sum(part.astype(f32), axis=0)[None]


def solution(mesh):
    mesh = Mesh(mesh.devices.reshape(N_KA, N_YH, N_YL, N_ZH, N_X), ("ka",) + PAIR)
    return jax.shard_map(
        shards,
        mesh=mesh,
        in_specs=(
            P("ka", PAIR, None),
            P("ka", PAIR),
            P(("ka",) + PAIR, None),
            P(("ka",) + PAIR),
            P("ka", PAIR, None),
            P("ka", PAIR),
        ),
        out_specs=P("ka", PAIR, None),
        check_vma=False,
    )
```

```python
import jax
import jax.numpy as jnp
from jax import lax
from jax.experimental import pallas as pl
from jax.experimental.pallas import tpu as pltpu
from jax.sharding import Mesh, PartitionSpec as P

BC = 128
GA = 16
GB = 128
WIN = 512
SLOTS = 16
GRID = 2048
NC = 8192
N_KA = 8
N_PAIR = 64
N_YH = 4
N_YL = 2
N_ZH = 2
N_X = 4
OWN = GRID // N_PAIR
PAIRS = SLOTS * BC
GROUP = 4
BLOCK = OWN + 2 * N_KA + N_KA
ENERGY = OWN + 2 * N_KA

PAIR = ("yh", "yl", "zh", "x")
NEAR = ("yl", "x")
FAR = ("yh", "zh")

f32 = jnp.float32
bf16 = jnp.bfloat16


def cosine_table(length):
    freq = lax.iota(jnp.float32, length)[:, None]
    point = lax.iota(jnp.float32, length)[None, :]
    factor = jnp.where(freq == 0, jnp.sqrt(1.0 / length), jnp.sqrt(2.0 / length))
    return (factor * jnp.cos(jnp.pi * (point + 0.5) * freq / length)).astype(jnp.bfloat16)


def vmem(count):
    return [pl.BlockSpec(memory_space=pltpu.VMEM)] * count


def params():
    return pltpu.CompilerParams(vmem_limit_bytes=48 * 2**20)


def piece_kernel(energy_ref, val_ref, slots_ref, out_ref, val_s, slots_s, sems):
    copies = [
        pltpu.make_async_copy(val_ref, val_s, sems.at[0]),
        pltpu.make_async_copy(slots_ref, slots_s, sems.at[1]),
    ]
    for copy in copies:
        copy.start()
    out_ref[...] = jnp.zeros_like(out_ref)
    for k in range(N_KA):
        out_ref[k, 2:3, :] = energy_ref[:1, :].astype(f32)
    for copy in copies:
        copy.wait()
    wanted = slots_s[...].astype(f32)
    for k in range(N_KA):
        for a in range(2):
            at = (2 * k + a) * GB
            out_ref[k, a:a + 1, :] = val_s[:, at:at + GB].astype(f32)
        out_ref[k, 3:4, :SLOTS] = wanted


def cond_kernel(cond_ref, out_ref):
    for d in range(N_PAIR):
        out_ref[d] = cond_ref[:, d * BC:(d + 1) * BC]


def pack_kernel(pieces_ref, cond_ref, out_ref):
    points = jnp.concatenate([pieces_ref[k, :2, :] for k in range(N_KA)], axis=0).astype(bf16)
    levels = jnp.concatenate([pieces_ref[k, 2:3, :] for k in range(N_KA)], axis=0).astype(bf16)
    for d in range(N_PAIR):
        out_ref[d, :OWN, :] = cond_ref[d]
        out_ref[d, OWN:ENERGY, :] = points
        out_ref[d, ENERGY:, :] = levels


def pick_kernel(slots_ref, got_ref, out_ref, rows_s, picked_s):
    for d in range(N_PAIR):
        rows_s[d] = got_ref[d, OWN:, :].astype(f32)
    for k in range(N_KA):
        for s in range(SLOTS):
            slot = slots_ref[k, s]
            owner = jnp.bitwise_and(slot, N_PAIR - 1)
            line = lax.shift_right_logical(slot, 6)
            for a in range(2):
                picked_s[k, a, s:s + 1, :] = rows_s[owner, pl.ds(2 * line + a, 1), :]
            picked_s[k, 2, s:s + 1, :] = rows_s[owner, pl.ds(2 * N_KA + line, 1), :]
    out_ref[...] = picked_s[...].astype(bf16)


def owner_slots(slots, got_ref, pick_ref, bd_ref, ta_ref, out_ref, first_s, moved_s, wtd_s, weight_s):
    def to_first(i, carry):
        cond = [got_ref[8 * i + t, :OWN, :].astype(f32) for t in range(8)]
        cond = [jnp.concatenate(cond[4 * h:4 * h + 4], axis=0) for h in range(2)]
        pick = [pick_ref[i, h].astype(f32).T for h in range(2)]
        for s0 in range(0, slots, GROUP):
            pair = [
                jnp.concatenate([cond[h] * pick[h][:, s:s + 1] for h in range(2)], axis=0).astype(bf16)
                for s in range(s0, s0 + GROUP)
            ]
            pair = jnp.concatenate(pair, axis=1)
            first = jnp.dot(bd_ref[...], pair, preferred_element_type=f32).astype(bf16)
            for h in range(2):
                for kg in range(8):
                    at = pl.multiple_of(kg * 256 + (2 * i + h) * 16, 16)
                    row = h * GB + kg * 16
                    first_s[pl.ds(at, 16), s0 * BC:(s0 + GROUP) * BC] = first[row:row + 16, :]
        return carry

    lax.fori_loop(0, 8, to_first, 0, unroll=4)

    def to_moved(kg, carry):
        start = pl.multiple_of(kg * 256, 256)
        for s0 in range(0, slots, GROUP):
            lanes = slice(s0 * BC, (s0 + GROUP) * BC)
            moved = jnp.dot(ta_ref[...], first_s[pl.ds(start, 256), lanes], preferred_element_type=f32)
            moved = moved.astype(bf16)
            for j in range(GA):
                at = pl.multiple_of(j * GB + kg * 16, 16)
                rows = moved[j * 16:j * 16 + 16, :]
                moved_s[pl.ds(at, 16), lanes] = rows
                if j < WIN // GB:
                    for t in range(GROUP):
                        s = s0 + t
                        part = rows[:, t * BC:(t + 1) * BC].astype(f32) * weight_s[s:s + 1, :]
                        wtd_s[pl.ds(at, 16), s * BC:(s + 1) * BC] = part.astype(bf16)
        return carry

    lax.fori_loop(0, 8, to_moved, 0, unroll=4)

    def to_out(i, carry):
        start = pl.multiple_of(i * 256, 256)
        total = lax.dot_general(
            moved_s[pl.ds(start, 256), :slots * BC], wtd_s[:, :slots * BC], (((1,), (1,)), ((), ())),
            preferred_element_type=f32,
        )
        total = (total * (2.0 / (SLOTS * BC * N_PAIR))).astype(bf16)
        for t in range(8):
            near = lax.rem(i, N_YL) * N_X + t % N_X
            far = lax.div(i, N_YL) * N_ZH + t // N_X
            out_ref[near, far] = total[t * OWN:(t + 1) * OWN]
        return carry

    lax.fori_loop(0, 8, to_out, 0, unroll=4)


def owner_kernel(count_ref, got_ref, pick_ref, e_cond_ref, bd_ref, ta_ref, out_ref,
                 first_s, moved_s, wtd_s, weight_s):
    count = count_ref[0]
    live = lax.broadcasted_iota(jnp.int32, (SLOTS, BC), 0) < count
    e_pick = pick_ref[0, 2].astype(f32)
    weight_s[...] = jnp.where(live, 1.0, 0.0) * 2.0 / (e_cond_ref[...] - e_pick)

    groups = jnp.clip(lax.div(count + GROUP - 1, GROUP), 1, SLOTS // GROUP)
    for slots in range(GROUP, SLOTS + GROUP, GROUP):
        @pl.when(groups * GROUP == slots)
        def _(slots=slots):
            owner_slots(slots, got_ref, pick_ref, bd_ref, ta_ref, out_ref,
                        first_s, moved_s, wtd_s, weight_s)


def shards(cond_orbitals, cond_energy, val_orbitals, val_energy, val_slots, owner_count):
    pieces = pl.pallas_call(
        piece_kernel,
        out_shape=jax.ShapeDtypeStruct((N_KA, 8, GB), f32),
        in_specs=vmem(1) + [pl.BlockSpec(memory_space=pl.ANY)] * 2,
        out_specs=vmem(1)[0],
        scratch_shapes=[
            pltpu.VMEM((1, GRID), bf16),
            pltpu.VMEM((1, SLOTS), jnp.int32),
            pltpu.SemaphoreType.DMA((2,)),
        ],
        compiler_params=pltpu.CompilerParams(vmem_limit_bytes=60 * 2**20),
        name="piece",
    )(jnp.broadcast_to(val_energy[:, None], (8, GB)), val_orbitals, val_slots[0])
    pieces = lax.all_to_all(pieces, "ka", 0, 0, tiled=True)
    slots = pieces[:, 3, :SLOTS].astype(jnp.int32)

    cond = pl.pallas_call(
        cond_kernel,
        out_shape=jax.ShapeDtypeStruct((N_PAIR, OWN, BC), bf16),
        in_specs=vmem(1),
        out_specs=vmem(1)[0],
        compiler_params=params(),
        name="cond",
    )(cond_orbitals[0])
    packed = pl.pallas_call(
        pack_kernel,
        out_shape=jax.ShapeDtypeStruct((N_PAIR, BLOCK, BC), bf16),
        in_specs=vmem(2),
        out_specs=vmem(1)[0],
        compiler_params=params(),
        name="pack",
    )(pieces, cond)
    got = lax.all_to_all(packed, PAIR, 0, 0, tiled=True)

    picked = pl.pallas_call(
        pick_kernel,
        out_shape=jax.ShapeDtypeStruct((N_KA, 3, SLOTS, GB), bf16),
        in_specs=[pl.BlockSpec(memory_space=pltpu.SMEM)] + vmem(1),
        out_specs=vmem(1)[0],
        scratch_shapes=[
            pltpu.VMEM((N_PAIR, BLOCK - OWN, GB), f32),
            pltpu.VMEM((N_KA, 3, SLOTS, GB), f32),
        ],
        compiler_params=params(),
        name="pick",
    )(slots, got)
    picked = lax.all_to_all(picked, "ka", 0, 0, tiled=True)

    bd = jnp.kron(jnp.eye(2, dtype=f32), cosine_table(GB).astype(f32)).astype(bf16)
    ta = jnp.kron(cosine_table(GA).astype(f32), jnp.eye(16, dtype=f32)).astype(bf16)
    part = pl.pallas_call(
        owner_kernel,
        out_shape=jax.ShapeDtypeStruct((N_YL * N_X, N_YH * N_ZH, OWN, WIN), bf16),
        in_specs=[pl.BlockSpec(memory_space=pltpu.SMEM)] + vmem(5),
        out_specs=vmem(1)[0],
        scratch_shapes=[
            pltpu.VMEM((GRID, PAIRS), bf16),
            pltpu.VMEM((GRID, PAIRS), bf16),
            pltpu.VMEM((WIN, PAIRS), bf16),
            pltpu.VMEM((SLOTS, BC), f32),
        ],
        compiler_params=params(),
        name="owner",
    )(owner_count[0], got, picked, cond_energy, bd, ta)

    part = lax.all_to_all(part, NEAR, 0, 0, tiled=True)
    part = jnp.sum(part.astype(f32), axis=0).astype(bf16)
    part = lax.all_to_all(part, FAR, 0, 0, tiled=True)
    return jnp.sum(part.astype(f32), axis=0)[None]


def solution(mesh):
    mesh = Mesh(mesh.devices.reshape(N_KA, N_YH, N_YL, N_ZH, N_X), ("ka",) + PAIR)
    return jax.shard_map(
        shards,
        mesh=mesh,
        in_specs=(
            P("ka", PAIR, None),
            P("ka", PAIR),
            P(("ka",) + PAIR, None),
            P(("ka",) + PAIR),
            P("ka", PAIR, None),
            P("ka", PAIR),
        ),
        out_specs=P("ka", PAIR, None),
        check_vma=False,
    )
```
